32 devices in a mesh: tm: 4 (over x, core), batch: 8 (over z, y).
Axes of the slice: x: 2, y: 2, z: 4, core: 2. Of those that a mesh axis runs over, the one named last changes fastest.
Arguments:
- inputs: bfloat16 [1536, 24, 100], P(('tm', 'batch')), may hold values from -6 to 6
- lengths: int32 [1536], P(('tm', 'batch')), may hold values from 5 to 21, as said below
- w_rec: bfloat16 [400, 400], P(None, 'tm'), may hold values from -0.3125 to 0.3125
- w_in: bfloat16 [100, 400], P(None, 'tm'), may hold values from -0.625 to 0.625
- rec_bias: float32 [400], replicated, may hold values from -3 to 3
- norm_gain: float32 [400], replicated, may hold values from 0.5 to 1.5
- norm_shift: float32 [400], replicated, may hold values from -2 to 2
- cotangent: bfloat16 [1536, 24, 400], P(('tm', 'batch')), may hold values from -6 to 6
Outputs:
- hidden: bfloat16 [1536, 24, 400], P(('tm', 'batch'))
- grad_inputs: float32 [1536, 24, 100], P(('tm', 'batch'))
- grad_w_rec: float32 [400, 400], P(None, 'tm')
- grad_w_in: float32 [100, 400], P(None, 'tm')
- grad_rec_bias: float32 [400], P('tm')
- grad_norm_gain: float32 [400], P('tm')
- grad_norm_shift: float32 [400], P('tm')
The draws below stay inside these ranges and needn't reach their ends.
Inputs may be any that keep to these rules, and one draw needn't show every extreme that they name: Steps t < lengths[b] are valid. In each aligned block of 48 sequences one has length 21 and the next (cyclically) length 5.
All inputs are finite; a program needn't handle non-finite values.
Results may differ from the reference program's by a relative error of at most 0.0053.
Values may be sent and summed in bfloat16 or wider, within the bound.
A program may use at most 256 MiB of HBM per device.

```python
import jax
import jax.numpy as jnp
from jax import lax

H = 400
E = 100
STEPS = 24
B_DEV = 48
LEAST = 5
LONGEST = 21
BATCH = 1536


def draw_lengths(key, part):
    key = jax.random.fold_in(key, 11)
    key_base, key_slot = jax.random.split(key)
    block_count = BATCH // B_DEV
    base_len = jax.random.randint(key_base, (block_count, B_DEV), LEAST, LONGEST + 1)
    long_slot = jax.random.randint(key_slot, (block_count, 1), 0, B_DEV)
    slot_ids = jnp.arange(B_DEV)[None, :]
    drawn_len = jnp.where(slot_ids == long_slot, LONGEST, jnp.where(slot_ids == (long_slot + 1) % B_DEV, LEAST, base_len))
    return drawn_len.reshape(BATCH).astype(jnp.int32)


def block_scale(key, shape, cuts, least, top_value):
    gain = 1.0
    for position, blocks in cuts:
        draws = jax.random.uniform(jax.random.fold_in(jax.random.fold_in(key, 6), position), (blocks,), jnp.float32, least / len(cuts), top_value / len(cuts))
        gain = gain * jnp.repeat(jnp.exp(draws), shape[position] // blocks).reshape((-1,) + (1,) * (len(shape) - 1 - position))
    return gain


def gaussian(key, shape, width, most, shards=(), held_as=jnp.bfloat16):
    factor_of = block_scale(key, shape, shards, -0.22, 0.18) if shards else 1.0
    entries = jax.random.normal(key, shape, jnp.float32) * width * factor_of
    return jnp.minimum(jnp.maximum(entries, -most), most).astype(held_as)


def setup_inputs(seed: int = 0) -> dict:
    key_list = jax.random.split(jax.random.key(seed), 9)
    return {
        "inputs": gaussian(key_list[0], (BATCH, STEPS, E), 1.0, 6.0, ((0, 32),)),
        "lengths": draw_lengths(jax.random.fold_in(key_list[8], 71), 0),
        "w_rec": gaussian(key_list[2], (H, H), H ** -0.5, 0.3125, ((1, 4),)),
        "w_in": gaussian(key_list[3], (E, H), E ** -0.5, 0.625, ((1, 4),)),
        "rec_bias": gaussian(key_list[4], (H,), 0.5, 3.0, (), jnp.float32),
        "norm_gain": jnp.clip(1.0 + 0.1 * jax.random.normal(key_list[5], (H,), jnp.float32), 0.5, 1.5),
        "norm_shift": gaussian(key_list[6], (H,), 0.3, 2.0, (), jnp.float32),
        "cotangent": gaussian(key_list[7], (BATCH, STEPS, H), 1.0, 6.0, ((0, 32),)),
    }


DECAY_RATE = 0.95
FAST_RATE = 0.5
NORM_EPS = 1e-05
EXACT = lax.Precision.HIGHEST

@jax.custom_vjp
def low(v):
    return lax.optimization_barrier(v.astype(jnp.bfloat16)).astype(jnp.float32)

@jax.custom_vjp
def low_back(v):
    return v

def low_keep(v):
    return (low(v), None)

def low_pass(kept, grad):
    return (grad,)

def back_keep(v):
    return (v, None)

def back_low(kept, grad):
    return (low(grad),)
low.defvjp(low_keep, low_pass)
low_back.defvjp(back_keep, back_low)

def norm_silu(mixed_pre, norm_gain, norm_shift):
    centre_mean = lax.optimization_barrier(jnp.mean(mixed_pre, -1, keepdims=True))
    centred = mixed_pre - centre_mean
    spread = lax.optimization_barrier(jnp.mean(centred * centred, -1, keepdims=True))
    return jax.nn.silu(centred * lax.rsqrt(spread + NORM_EPS) * norm_gain + norm_shift)

def forward_group(x_group, in_seq, w_rec, w_in, rec_bias, norm_gain, norm_shift):
    group_rows = x_group.shape[0]
    hidden_width = w_rec.shape[0]

    def cell_step(carry_pair, step_item):
        state_a, state_h = carry_pair
        x_now, keep_now = step_item
        pre_act = low_back(jnp.dot(low(state_h), w_rec, precision=EXACT, preferred_element_type=jnp.float32) + jnp.dot(x_now, w_in, precision=EXACT, preferred_element_type=jnp.float32) + rec_bias)
        first_act = jax.nn.silu(pre_act)
        grown_a = DECAY_RATE * state_a + FAST_RATE * state_h[:, :, None] * state_h[:, None, :]
        mixed_pre = pre_act + jnp.einsum('gpq,gq->gp', grown_a, first_act, precision=EXACT)
        out_act = norm_silu(mixed_pre, norm_gain, norm_shift)
        new_h = jnp.where(keep_now[:, None], out_act, state_h)
        new_a = jnp.where(keep_now[:, None, None], grown_a, state_a)
        return ((new_a, new_h), new_h)
    start_pair = (jnp.zeros((group_rows, hidden_width, hidden_width), jnp.float32), jnp.zeros((group_rows, hidden_width), jnp.float32))
    _, states = lax.scan(jax.checkpoint(cell_step), start_pair, (jnp.swapaxes(x_group, 0, 1), jnp.swapaxes(in_seq, 0, 1)))
    return jnp.swapaxes(states, 0, 1)

def reference(inputs, lengths, w_rec, w_in, rec_bias, norm_gain, norm_shift, cotangent):
    group_count = BATCH // B_DEV
    x_groups = inputs.astype(jnp.float32).reshape(group_count, B_DEV, STEPS, E)
    cot_groups = cotangent.astype(jnp.float32).reshape(group_count, B_DEV, STEPS, H)
    len_groups = lengths.reshape(group_count, B_DEV)
    params = (w_rec.astype(jnp.float32), w_in.astype(jnp.float32), rec_bias, norm_gain, norm_shift)

    def one_group(running, group_item):
        x_group, len_group, cot_group = group_item
        in_seq = jnp.arange(STEPS, dtype=jnp.int32)[None, :] < len_group[:, None]

        def run_cell(x_in, a, b, c, d, e):
            return forward_group(x_in, in_seq, a, b, c, d, e)
        states, pull_back = jax.vjp(run_cell, x_group, *params)
        grads = pull_back(cot_group)
        running = tuple((total + piece for total, piece in zip(running, grads[1:])))
        return (running, (states.astype(jnp.bfloat16), grads[0]))
    start_sums = tuple((jnp.zeros_like(param) for param in params))
    totals, (states, grad_x) = lax.scan(one_group, start_sums, (x_groups, len_groups, cot_groups))
    return (states.reshape(BATCH, STEPS, H), grad_x.reshape(BATCH, STEPS, E), totals[0], totals[1], totals[2], totals[3], totals[4])
```

```python
import functools, math
import jax, jax.numpy as jnp
from jax import lax
from jax.experimental import pallas as pl
from jax.experimental.pallas import tpu as pltpu
from jax.sharding import PartitionSpec as P
F32, BF16 = jnp.float32, jnp.bfloat16
DECAY, RATE, EPS = 0.95, 0.5, 1e-5
B, T, TV, H, E = 48, 24, 21, 400, 100
HP = 512
LT = H // 128 * 128
OFF = H - LT
SUB = 8

def kappa(i):
    return math.sqrt(RATE) * DECAY ** (-i / 2)

def body(cfg, x_ref, len_ref, cot_ref, wc_ref, gain_ref, shift_ref,
         hid_out, gx_out, g_out,
         xs, xr, cotf, hidf, hx, first_s, slope_s, s_s, xh_s, rstd_s, pt_s, pc_s, f_s, dpre_s, dmix_s, mt_s, gain_acc, shift_acc, gain_p, shift_p):
    chains = cfg["chains"]
    NG = B // SUB
    lane = lax.broadcasted_iota(jnp.int32, (SUB, 128), 1)
    hmask = (lax.broadcasted_iota(jnp.int32, (SUB, HP), 1) < H)
    xs[:, :E] = x_ref[...].astype(F32)
    def prep(i, _):
        r = pl.ds(pl.multiple_of(i * 48, 48), 48)
        v = pltpu.roll(xs[r, :], OFF, 1)
        l = lax.broadcasted_iota(jnp.int32, (48, 128), 1)
        xr[r, :] = jnp.where(l < OFF + E, v, jnp.where(l < OFF + E + 3, 1.0, 0.0))
        for k in range(3):
            cotf[k, r, :] = cot_ref[r, k * 128:(k + 1) * 128].astype(F32)
        cotf[3, r, :] = jnp.zeros((48, 128), F32)
        cotf[3, r, :OFF] = cot_ref[r, LT:].astype(F32)
        return 0
    lax.fori_loop(0, B * T // 48, prep, 0)
    zero8 = jnp.zeros((SUB, HP), F32)
    for padded, ref in ((gain_p, gain_ref), (shift_p, shift_ref)):
        padded[...] = jnp.zeros((SUB, HP), F32)
        padded[:, :H] = jnp.broadcast_to(ref[...], (SUB, H))
    gain, shift = gain_p[...], shift_p[...]
    lens = [jnp.broadcast_to(len_ref[g * SUB:(g + 1) * SUB, :], (SUB, 128)) for g in range(NG)]
    def valid(g, t):
        m = lens[g] > t
        return jnp.concatenate([m] * 4, 1)
    def bl(c):
        return jnp.broadcast_to(c, (SUB, HP))
    def rows(g): return slice(g * SUB, (g + 1) * SUB)
    h = [zero8] * NG
    for t in range(TV):
        dec = DECAY ** t
        for r0, nr in chains:
            gs = range(r0 // SUB, (r0 + nr) // SUB)
            xt = xr[pl.ds(r0 * T + t, nr, stride=T), :]
            hv = jnp.concatenate([h[g] for g in gs], 0)
            l = lax.broadcasted_iota(jnp.int32, (nr, 128), 1)
            hv = jnp.concatenate([hv[:, :LT], jnp.where(l < OFF, hv[:, LT:], xt)], 1).astype(BF16)
            hx[t * B + r0: t * B + r0 + nr, :] = hv
            if t == 0:
                u = jnp.dot(hv[:, LT:], wc_ref[LT:, :], preferred_element_type=F32)
            else:
                u = jnp.dot(hv, wc_ref[...], preferred_element_type=F32)
            cs = {}
            us = {}
            for k, g in enumerate(gs):
                ug = u[k * SUB:(k + 1) * SUB, :]
                us[g] = ug
                sg = jax.nn.sigmoid(ug)
                first = ug * sg
                slope_s[t, rows(g), :] = (sg + first * (1.0 - sg)) * dec
                first = first * dec
                first_s[t, rows(g), :] = first
                cs[g] = []
                for i in range(1, t + 1):
                    c = jnp.sum(pt_s[i, rows(g), :] * first, -1, keepdims=True)
                    f_s[t * (t - 1) // 2 + i - 1, rows(g), :] = jnp.broadcast_to(c, (SUB, 128))
                    cs[g].append(c)
            for k, g in enumerate(gs):
                ug = us[g]
                mu = jnp.sum(ug, -1, keepdims=True) * (1.0 / H)
                mc = jnp.where(hmask, ug - bl(mu), 0.0)
                for i in range(1, t + 1):
                    mc = mc + bl(cs[g][i - 1]) * pc_s[i, rows(g), :]
                var = jnp.sum(mc * mc, -1, keepdims=True) * (1.0 / H)
                rstd = lax.rsqrt(var + EPS)
                xh = mc * bl(rstd)
                z = xh * gain + shift
                sz = jax.nn.sigmoid(z)
                out = z * sz
                xh_s[t, rows(g), :] = xh
                rstd_s[t, rows(g), :] = jnp.broadcast_to(rstd, (SUB, 128))
                s_s[t, rows(g), :] = sz + out * (1.0 - sz)
                h[g] = jnp.where(valid(g, t), out, h[g])
                for tt in ([t] if t < TV - 1 else range(t, T)):
                    for k4 in range(4):
                        hidf[k4, pl.ds(g * SUB * T + tt, SUB, stride=T), :] = h[g][:, k4 * 128:(k4 + 1) * 128]
                if t < TV - 1:
                    pt = h[g] * kappa(t + 1)
                    pt_s[t + 1, rows(g), :] = pt
                    mp = jnp.sum(pt, -1, keepdims=True) * (1.0 / H)
                    pc_s[t + 1, rows(g), :] = jnp.where(hmask, pt - bl(mp), 0.0)
    def cot(g, t):
        return jnp.concatenate([cotf[k, pl.ds(g * SUB * T + t, SUB, stride=T), :] for k in range(4)], 1)
    grad = []
    for g in range(NG):
        a = cot(g, T - 1)
        for t in range(T - 2, TV - 1, -1):
            a = a + cot(g, t)
        grad.append(a)
        gain_acc[rows(g), :] = jnp.zeros((SUB, HP), F32)
        shift_acc[rows(g), :] = jnp.zeros((SUB, HP), F32)
    for t in range(TV - 1, -1, -1):
        for r0, nr in chains:
            gs = range(r0 // SUB, (r0 + nr) // SUB)
            passed, dmixs, ms, dpres = {}, {}, {}, {}
            for g in gs:
                tot = grad[g] + cot(g, t)
                D = jnp.where(valid(g, t), tot, 0.0)
                passed[g] = tot
                xh = xh_s[t, rows(g), :]
                dz = D * s_s[t, rows(g), :]
                gain_acc[rows(g), :] += dz * xh
                shift_acc[rows(g), :] += dz
                dxh = dz * gain
                m1 = jnp.sum(dxh, -1, keepdims=True) * (1.0 / H)
                m2 = jnp.sum(dxh * xh, -1, keepdims=True) * (1.0 / H)
                rstd = rstd_s[t, rows(g), :]
                dmix = jnp.concatenate([rstd] * 4, 1) * (dxh - bl(m1) - xh * bl(m2))
                dmixs[g] = dmix
                dmix_s[t, rows(g), :] = dmix
            for g in gs:
                ms[g] = []
                for i in range(1, t + 1):
                    c = jnp.sum(pt_s[i, rows(g), :] * dmixs[g], -1, keepdims=True)
                    ms[g].append(c)
                    mt_s[t * (t - 1) // 2 + i - 1, rows(g), :] = jnp.broadcast_to(c, (SUB, 128))
            for g in gs:
                if t > 0:
                    df = bl(ms[g][0]) * pt_s[1, rows(g), :]
                    for i in range(2, t + 1):
                        df = df + bl(ms[g][i - 1]) * pt_s[i, rows(g), :]
                    dpres[g] = dmixs[g] + df * slope_s[t, rows(g), :]
                else:
                    dpres[g] = dmixs[g]
            dp = jnp.concatenate([dpres[g] for g in gs], 0).astype(BF16)
            dpre_s[t * B + r0: t * B + r0 + nr, :] = dp
            fr = lax.dot_general(dp, wc_ref[...] if t > 0 else wc_ref[LT:, :], (((1,), (1,)), ((), ())), preferred_element_type=F32)
            gxt = fr[:, -128:]
            xs[pl.ds(r0 * T + t, nr, stride=T), :] = pltpu.roll(gxt, 128 - OFF, 1)
            if t > 0:
                for k, g in enumerate(gs):
                    S = None
                    for kk in range(TV - 1, t - 1, -1):
                        q = kk * (kk - 1) // 2 + t - 1
                        fc = f_s[q, rows(g), :]
                        mc_ = mt_s[q, rows(g), :] if kk > t else ms[g][t - 1]
                        fc = jnp.concatenate([fc] * 4, 1)
                        mc_ = jnp.concatenate([mc_] * 4, 1) if kk > t else bl(mc_)
                        term = fc * (dmix_s[kk, rows(g), :] if kk > t else dmixs[g]) + mc_ * first_s[kk, rows(g), :]
                        S = term if S is None else S + term
                    new = fr[k * SUB:(k + 1) * SUB, :] + S * kappa(t)
                    grad[g] = jnp.where(valid(g, t), new, passed[g])
        if t % 5 == 1:
            a = hx[t * B:(t + 5) * B, :]
            d = dpre_s[t * B:(t + 5) * B, :]
            prod = lax.dot_general(a, d, (((0,), (0,)), ((), ())), preferred_element_type=F32)
            if t + 5 == TV:
                g_out[...] = prod
            else:
                g_out[...] += prod
        if t == 0:
            prod = lax.dot_general(hx[:B, LT:], dpre_s[:B, :], (((0,), (0,)), ((), ())), preferred_element_type=F32)
            g_out[LT:, :] += prod
    g_out[HP - 8:, :] = jnp.concatenate([
        g_out[HP - 8:HP-7,:]*0, g_out[HP - 7:HP-6,:]*0,
        jnp.sum(gain_acc[...], 0, keepdims=True), jnp.sum(shift_acc[...], 0, keepdims=True), jnp.zeros((4, HP), F32)], 0)
    for t in range(TV, T):
        xs[pl.ds(t, B, stride=T), :] = jnp.zeros((B, 128), F32)
    def fin(i, _):
        r = pl.ds(pl.multiple_of(i * 48, 48), 48)
        for k in range(3):
            hid_out[r, k * 128:(k + 1) * 128] = hidf[k, r, :].astype(BF16)
        hid_out[r, LT:] = hidf[3, r, :OFF].astype(BF16)
        gx_out[r, :] = xs[r, :E]
        return 0
    lax.fori_loop(0, B * T // 48, fin, 0)


MESH = pl.DeviceIdType.MESH


def gather_body(w_ref, c_ref, bias_ref, wc_out, blk, brow, ssem, xsem, fsem, rsem, xrsem, frsem):
    me, b = lax.axis_index("tm"), lax.axis_index("batch")
    sib, xp = lax.bitwise_xor(me, 1), lax.bitwise_xor(me, 2)
    diag = lax.bitwise_xor(me, 3)
    barrier = pltpu.get_barrier_semaphore()
    for peer in (sib, xp):
        pl.semaphore_signal(barrier, inc=1, device_id=(peer, b), device_id_type=MESH)
    blk[me] = jnp.zeros((HP, 128), BF16)
    blk[me, :H, :E] = w_ref[...]
    blk[me, H:H + E, :E] = c_ref[...]
    brow[...] = jnp.zeros((SUB, HP), F32)
    brow[:1, :H] = bias_ref[...]
    pl.semaphore_wait(barrier, 2)
    def half(ref_slot, i):
        return blk.at[ref_slot, pl.ds(i * 256, 256)]
    xcopies = []
    for i in range(2):
        cp = pltpu.make_async_remote_copy(src_ref=half(me, i), dst_ref=half(me, i), send_sem=xsem.at[i], recv_sem=xrsem.at[i],
            device_id=(xp, b), device_id_type=MESH)
        cp.start()
        xcopies.append(cp)
    own = pltpu.make_async_remote_copy(src_ref=blk.at[me], dst_ref=blk.at[me], send_sem=ssem, recv_sem=rsem,
        device_id=(sib, b), device_id_type=MESH)
    own.start()
    fcopies = []
    for i in range(2):
        xcopies[i].wait_recv()
        cp = pltpu.make_async_remote_copy(src_ref=half(xp, i), dst_ref=half(xp, i), send_sem=fsem.at[i], recv_sem=frsem.at[i],
            device_id=(sib, b), device_id_type=MESH)
        cp.start()
        fcopies.append(cp)
    own.wait_recv()
    for i in range(2):
        fcopies[i].wait_recv()
    own.wait_send()
    for i in range(2):
        xcopies[i].wait_send()
        fcopies[i].wait_send()
    row = lax.broadcasted_iota(jnp.int32, (16, HP), 0)
    bias = jnp.broadcast_to(brow[:1, :], (16, HP))
    hi = bias.astype(BF16).astype(F32)
    mid = (bias - hi).astype(BF16).astype(F32)
    lo = bias - hi - mid
    for r in range(0, HP, 64):
        l = lax.broadcasted_iota(jnp.int32, (64, 128), 1)
        b0, b1, b2, b3 = [blk[k, r:r + 64, :].astype(F32) for k in range(4)]
        b1, b2, b3 = pltpu.roll(b1, 100, 1), pltpu.roll(b2, 72, 1), pltpu.roll(b3, 44, 1)
        wc_out[r:r + 64, 0:128] = jnp.where(l < 100, b0, b1).astype(BF16)
        wc_out[r:r + 64, 128:256] = jnp.where(l < 72, b1, b2).astype(BF16)
        wc_out[r:r + 64, 256:384] = jnp.where(l < 44, b2, b3).astype(BF16)
        wc_out[r:r + 64, 384:512] = jnp.where(l < 16, b3, 0.0).astype(BF16)
    last = wc_out[HP - 16:, :].astype(F32)
    last = jnp.where(row == 4, hi, jnp.where(row == 5, mid, jnp.where(row == 6, lo, jnp.where(row < 4, last, 0.0))))
    wc_out[HP - 16:, :] = last.astype(BF16)


def gather_call(w, c, bias):
    D = pltpu.SemaphoreType.DMA
    return pl.pallas_call(
        gather_body,
        out_shape=jax.ShapeDtypeStruct((HP, HP), BF16),
        scratch_shapes=[pltpu.VMEM((4, HP, 128), BF16), pltpu.VMEM((SUB, HP), F32), D, D((2,)), D((2,)), D, D((2,)), D((2,))],
        compiler_params=pltpu.CompilerParams(collective_id=0, has_side_effects=True, vmem_limit_bytes=60 * 2**20),
    )(w, c, bias.reshape(1, H))


def reduce_body(nb, g_ref, gw_out, gc_out, v_out, blk, pk, sib_in, rs_out, rs_in, ag, ssem, srsem, rsem_s, rsem_r, asem_s, asem_r):
    me, b = lax.axis_index("tm"), lax.axis_index("batch")
    core, sib = lax.rem(me, 2), lax.bitwise_xor(me, 1)
    xi = me // 2
    piece = HP // nb
    barrier = pltpu.get_barrier_semaphore()
    pl.semaphore_signal(barrier, inc=1, device_id=(sib, b), device_id_type=MESH)
    others = [(dx, db) for db in range(nb) for dx in range(2) if dx or db]
    base = b // nb * nb
    rank = b - base
    def peer(dx, db):
        return lax.rem(xi + dx, 2), base + lax.rem(rank + db, nb)
    for dx, db in others:
        px, pb = peer(dx, db)
        pl.semaphore_signal(barrier, inc=1, device_id=(2 * px + core, pb), device_id_type=MESH)
    l = lax.broadcasted_iota(jnp.int32, (64, 128), 1)
    for r in range(0, HP, 64):
        t0, t1, t2, t3 = [g_ref[r:r + 64, k * 128:(k + 1) * 128] for k in range(4)]
        out = [t0,
            jnp.where(l < 28, pltpu.roll(t0, 28, 1), pltpu.roll(t1, 28, 1)),
            jnp.where(l < 56, pltpu.roll(t1, 56, 1), pltpu.roll(t2, 56, 1)),
            jnp.where(l < 84, pltpu.roll(t2, 84, 1), pltpu.roll(t3, 84, 1))]
        for k in range(4):
            blk[k, r:r + 64, :] = out[k]
            pk[k, r:r + 64, :] = out[k].astype(BF16)
    pl.semaphore_wait(barrier, len(others) + 1)
    scopies = []
    for j in range(2):
        k = 2 * j + (1 - core)
        cp = pltpu.make_async_remote_copy(src_ref=pk.at[k], dst_ref=sib_in.at[j], send_sem=ssem.at[j], recv_sem=srsem.at[j],
            device_id=(sib, b), device_id_type=MESH)
        cp.start()
        scopies.append(cp)
    for j in range(2):
        scopies[j].wait_recv()
        for r in range(0, HP, 64):
            rs_out[j, r:r + 64, :] = (blk[2 * j + core, r:r + 64, :] + sib_in[j, r:r + 64, :].astype(F32)).astype(BF16)
    rcopies = []
    for n, (dx, db) in enumerate(others):
        px, pb = peer(dx, db)
        slot = dx * nb + db
        cp = pltpu.make_async_remote_copy(src_ref=rs_out.at[px, pl.ds(pl.multiple_of((pb - base) * piece, piece), piece)], dst_ref=rs_in.at[slot],
            send_sem=rsem_s.at[slot], recv_sem=rsem_r.at[slot], device_id=(2 * px + core, pb), device_id_type=MESH)
        cp.start()
        rcopies.append(cp)
    total = rs_out[xi, pl.ds(pl.multiple_of(rank * piece, piece), piece), :].astype(F32)
    for n, (dx, db) in enumerate(others):
        rcopies[n].wait_recv()
        total = total + rs_in[dx * nb + db].astype(F32)
    ag[rank] = total.astype(BF16)
    acopies = []
    for db in range(1, nb):
        pb = base + lax.rem(rank + db, nb)
        cp = pltpu.make_async_remote_copy(src_ref=ag.at[rank], dst_ref=ag.at[rank], send_sem=asem_s.at[db], recv_sem=asem_r.at[db],
            device_id=(me, pb), device_id_type=MESH)
        cp.start()
        acopies.append(cp)
    for cp in acopies:
        cp.wait_recv()
    for j in range(nb):
        v = ag[j].astype(F32)
        for r in range(0, piece, 8):
            row = j * piece + r
            blk[0, row:row + 8, :] = v[r:r + 8, :]
    gw_out[...] = blk[0, :H, :E]
    gc_out[...] = blk[0, H:H + E, :E]
    v_out[...] = blk[0, HP - 16:, :E]
    for cp in scopies + rcopies + acopies:
        cp.wait_send()


def reduce_call(g, nb):
    D = pltpu.SemaphoreType.DMA
    V = pltpu.VMEM
    piece = HP // nb
    return pl.pallas_call(
        functools.partial(reduce_body, nb),
        out_shape=(jax.ShapeDtypeStruct((H, E), F32), jax.ShapeDtypeStruct((E, E), F32), jax.ShapeDtypeStruct((16, E), F32)),
        scratch_shapes=[V((4, HP, 128), F32), V((4, HP, 128), BF16), V((2, HP, 128), BF16), V((2, HP, 128), BF16),
            V((2 * nb, piece, 128), BF16), V((nb, piece, 128), BF16),
            D((2,)), D((2,)), D((2 * nb,)), D((2 * nb,)), D((nb,)), D((nb,))],
        compiler_params=pltpu.CompilerParams(collective_id=1, has_side_effects=True, vmem_limit_bytes=60 * 2**20),
    )(g)


def cell_call(x, lengths, cot, wc, gain, shift):
    NP = TV * (TV - 1) // 2
    V = pltpu.VMEM
    return pl.pallas_call(
        functools.partial(body, dict(chains=[(0, 16), (16, 16), (32, 16)])),
        out_shape=(jax.ShapeDtypeStruct((B * T, H), BF16), jax.ShapeDtypeStruct((B * T, E), F32), jax.ShapeDtypeStruct((HP, HP), F32)),
        scratch_shapes=[V((B * T, 128), F32), V((B * T, 128), F32), V((4, B * T, 128), F32), V((4, B * T, 128), F32),
            V((TV * B, HP), BF16), V((TV, B, HP), F32), V((TV, B, HP), F32), V((TV, B, HP), F32), V((TV, B, HP), F32), V((TV, B, 128), F32),
            V((TV, B, HP), F32), V((TV, B, HP), F32), V((NP, B, 128), F32), V((TV * B, HP), BF16), V((TV, B, HP), F32), V((NP, B, 128), F32),
            V((B, HP), F32), V((B, HP), F32), V((SUB, HP), F32), V((SUB, HP), F32)],
        compiler_params=pltpu.CompilerParams(vmem_limit_bytes=60 * 2**20),
    )(x.reshape(B * T, E), lengths.reshape(B, 1), cot.reshape(B * T, H), wc, gain.reshape(1, H), shift.reshape(1, H))


def per_device(inputs, lengths, w_rec, w_in, rec_bias, norm_gain, norm_shift, cotangent, nb):
    wc = gather_call(w_rec, w_in, rec_bias)
    hid, gx, g = cell_call(inputs, lengths, cotangent, wc, norm_gain, norm_shift)
    group = math.gcd(nb, 8)
    parts = reduce_call(g, group)
    if nb > group:
        parts = [lax.all_gather(p, "batch").reshape(nb // group, group, *p.shape)[:, 0].sum(0) for p in parts]
    gw, gc, v = parts
    return hid.reshape(B, T, H), gx.reshape(B, T, E), gw, gc, v[4], v[10], v[11]


def solution(mesh):
    both = ("tm", "batch")
    return jax.shard_map(
        functools.partial(per_device, nb=mesh.shape["batch"]),
        mesh=mesh,
        in_specs=(P(both, None, None), P(both), P(None, "tm"), P(None, "tm"), P(), P(), P(), P(both, None, None)),
        out_specs=(P(both, None, None), P(both, None, None), P(None, "tm"), P(None, "tm"), P("tm"), P("tm"), P("tm")),
        check_vma=False,
    )
```

```python
import functools, math
import jax, jax.numpy as jnp
from jax import lax
from jax.experimental import pallas as pl
from jax.experimental.pallas import tpu as pltpu
from jax.sharding import PartitionSpec as P
F32, BF16 = jnp.float32, jnp.bfloat16
DECAY, RATE, EPS = 0.95, 0.5, 1e-5
B, T, TV, H, E = 48, 24, 21, 400, 100
HP = 512
NT = 4
LT = H // 128 * 128
OFF = H - LT
SUB = 8
ROWS = 16
NC = B // ROWS
NP = TV * (TV - 1) // 2
ONES = 3
LEAST = 5

def kappa(i):
    return math.sqrt(RATE) * DECAY ** (-i / 2)

def tri(t, i):
    return t * (t - 1) // 2 + i - 1

PLANS = ((21, 21, 19, 17, 14, 11), (TV,) * (B // SUB))


def cell_body(info, xs_in, lens_ref, cotf_in, wc_ref, gain_p, shift_p, hid_out, gx_out, hx, dpre_s, sums_out, xs, cotf, gxs, hidf, h_s, *rest):
    accs = [pltpu.ACC(m)((ROWS, 256), F32) for _ in range(NC) for m in range(2)]
    def place(row, n):
        return pl.ds(pl.multiple_of(info[row, n] * T, SUB), T)
    for r in range(B):
        xs[r * T:(r + 1) * T, :] = xs_in[place(1, r), :]
    h_s[...] = jnp.zeros((B, HP), F32)
    sums_out[...] = jnp.zeros((2 * SUB, HP), F32)
    def scoped(*a):
        def run(ends):
            cell_inner(ends, place, xs, lens_ref, cotf_in, wc_ref, gain_p, shift_p, hid_out, hx, dpre_s, sums_out,
                cotf, gxs, hidf, h_s, *rest, [a[2 * i:2 * i + 2] for i in range(NC)])
        lax.cond(info[2, 0] > 0, lambda: run(PLANS[0]), lambda: run(PLANS[1]))
    pl.run_scoped(scoped, *accs)
    for b in range(B):
        gx_out[b * T:(b + 1) * T, :] = gxs[place(0, b), :E]


def cell_inner(ends, place, xs, lens_ref, cotf_in, wc_ref, gain_p, shift_p, hid_out, hx, dpre_s, sums_out,
        cotf, gxs, hidf, h_s, grad_s, first_s, slope_s, s_s, xh_s, rstd_s, pt_s, pc_s, f_s, mt_s, dmix_s, accs):
    lane = lax.broadcasted_iota(jnp.int32, (SUB, 128), 1)
    lane16 = lax.broadcasted_iota(jnp.int32, (ROWS, 128), 1)
    tail = lane < OFF
    zero = jnp.zeros((SUB, 128), F32)
    zb = jnp.zeros((ROWS, HP), BF16)
    def chains(t): return [c for c in range(NC) if ends[2 * c] > t]
    def groups(c, t): return [g for g in (2 * c, 2 * c + 1) if ends[g] > t]
    def rows(g): return slice(g * SUB, (g + 1) * SUB)
    def crow(c): return slice(c * ROWS, (c + 1) * ROWS)
    def cut(k): return slice(k * 128, (k + 1) * 128)
    def ld(ref, t, g): return [ref[t, rows(g), cut(k)] for k in range(NT)]
    def st(ref, t, g, v):
        for k in range(NT):
            ref[t, rows(g), cut(k)] = v[k]
    def lsum(v):
        return jnp.broadcast_to(jnp.sum((v[0] + v[1]) + (v[2] + v[3]), -1, keepdims=True), (SUB, 128))
    def only_h(v): return [v[0], v[1], v[2], jnp.where(tail, v[3], 0.0)]
    def push(k, transpose):
        for m in range(2):
            if transpose:
                w = wc_ref[m * 256:(m + 1) * 256, k * 256:(k + 1) * 256]
            else:
                w = wc_ref[k * 256:(k + 1) * 256, m * 256:(m + 1) * 256]
            pltpu.matmul_push_rhs(w, k, m, transpose=transpose)
    def mm(c, v, transpose, last, after):
        lhs = [jnp.concatenate(v[:2], 1), jnp.concatenate(v[2:], 1)]
        o = (0, 1) if c % 2 == 0 else (1, 0)
        for n, k in enumerate(o):
            for m in range(2):
                pltpu.matmul_acc_lhs(accs[c][m], lhs[k], load_staged_rhs=k if n or c == 0 else None)
            if n == 0 and c > 0:
                push(o[1], transpose)
        if last and after is not None:
            push(0, after), push(1, after)
    def pop(c):
        u = [pltpu.matmul_pop(accs[c][m]) for m in range(2)]
        return [u[0][:, :128], u[0][:, 128:], u[1][:, :128], u[1][:, 128:]]
    push(0, False), push(1, False)
    def sort_cot(r):
        for k in range(NT):
            cotf[k, r * T:(r + 1) * T, :] = cotf_in[k, place(1, r), :]
    def fin(i):
        r = slice(i * 2 * T, (i + 1) * 2 * T)
        for k in range(NT):
            v = jnp.concatenate([hidf[k, place(0, 2 * i + j), :] for j in range(2)], 0).astype(BF16)
            hid_out[r, k * 128:min((k + 1) * 128, H)] = v[:, :min(128, H - k * 128)]
    def live(g, t):
        return lens_ref[rows(g), :] > t
    def seqs(c, t): return pl.ds(c * ROWS * T + t, ROWS, stride=T)
    def gseqs(g, t): return pl.ds(g * SUB * T + t, SUB, stride=T)
    def step_rows(c, t): return slice(t * B + c * ROWS, t * B + (c + 1) * ROWS)

    def fwd_step(t):
        dec = DECAY ** t
        on = chains(t)
        for c in range(NC):
            if c not in on:
                hx[step_rows(c, t), :] = zb
                continue
            hv = [h_s[crow(c), cut(k)] for k in range(NT)]
            hv[3] = jnp.where(lane16 < OFF, hv[3], xs[seqs(c, t), :])
            hb = [v.astype(BF16) for v in hv]
            for k in range(NT):
                hx[step_rows(c, t), cut(k)] = hb[k]
            mm(c, hb, False, c == on[-1], t == TV - 1)
        if t > 0:
            for c in on:
                for g in groups(c, t):
                    pt = [h_s[rows(g), cut(k)] * kappa(t) for k in range(NT)]
                    st(pt_s, t, g, pt)
                    mp = lsum(pt) * (1.0 / H)
                    st(pc_s, t, g, only_h([v - mp for v in pt]))
        for c in on:
            u16 = pop(c)
            cs, us = {}, {}
            for g in groups(c, t):
                j = g - 2 * c
                u = [v[j * SUB:(j + 1) * SUB, :] for v in u16]
                mu = lsum(u) * (1.0 / H)
                us[g] = only_h([v - mu for v in u])
                sg = [jax.nn.sigmoid(v) for v in u]
                sgd = [v * dec for v in sg]
                first = [a * b for a, b in zip(u, sgd)]
                st(first_s, t, g, first)
                st(slope_s, t, g, [a + f - f * s for a, f, s in zip(sgd, first, sg)])
                cs[g] = []
                for i in range(1, t + 1):
                    cc = lsum([a * b for a, b in zip(ld(pt_s, i, g), first)])
                    f_s[tri(t, i), rows(g), :] = cc
                    cs[g].append(cc)
            for g in groups(c, t):
                mc = us[g]
                for i in range(1, t + 1):
                    mc = [m + cs[g][i - 1] * p for m, p in zip(mc, ld(pc_s, i, g))]
                var = lsum([m * m for m in mc]) * (1.0 / H)
                rstd = lax.rsqrt(var + EPS)
                xh = [m * rstd for m in mc]
                z = [x * gain_p[:, cut(k)] + shift_p[:, cut(k)] for k, x in enumerate(xh)]
                sz = [jax.nn.sigmoid(v) for v in z]
                out = [a * b for a, b in zip(z, sz)]
                new = out
                if t >= LEAST:
                    ok = live(g, t)
                    new = [jnp.where(ok, a, h_s[rows(g), cut(k)]) for k, a in enumerate(out)]
                for k in range(NT):
                    h_s[rows(g), cut(k)] = new[k]
                    for tt in [t] if t < ends[g] - 1 else range(t, T):
                        hidf[k, gseqs(g, tt), :] = new[k]
                st(xh_s, t, g, xh)
                rstd_s[t, rows(g), :] = rstd
                st(s_s, t, g, [a + o - o * a for a, o in zip(sz, out)])

    def bwd_step(t):
        on = chains(t)
        sums = [None, None]
        dmixs, tots, ms = {}, {}, {}
        for c in range(NC):
            if c not in on:
                dpre_s[step_rows(c, t), :] = zb
                gxs[seqs(c, t), :] = jnp.zeros((ROWS, 128), F32)
                continue
            dps = [[zero] * NT, [zero] * NT]
            for g in groups(c, t):
                if t == ends[g] - 1:
                    tot = [cotf[k, gseqs(g, T - 1), :] for k in range(NT)]
                    for tt in range(T - 2, t - 1, -1):
                        tot = [a + cotf[k, gseqs(g, tt), :] for k, a in enumerate(tot)]
                else:
                    tot = [grad_s[rows(g), cut(k)] + cotf[k, gseqs(g, t), :] for k in range(NT)]
                tots[g] = tot
                xh = ld(xh_s, t, g)
                d = tot if t < LEAST else [jnp.where(live(g, t), a, 0.0) for a in tot]
                dz = [a * s for a, s in zip(d, ld(s_s, t, g))]
                gs = [a * b for a, b in zip(dz, xh)]
                sums = [gs, dz] if sums[0] is None else [[a + b for a, b in zip(p, q)] for p, q in zip(sums, (gs, dz))]
                dxh = [a * gain_p[:, cut(k)] for k, a in enumerate(dz)]
                m1 = lsum(dxh) * (1.0 / H)
                m2 = lsum([a * b for a, b in zip(dxh, xh)]) * (1.0 / H)
                rstd = rstd_s[t, rows(g), :]
                dmixs[g] = only_h([rstd * (a - m1 - b * m2) for a, b in zip(dxh, xh)])
                st(dmix_s, t, g, dmixs[g])
            for g in groups(c, t):
                ms[g] = []
                for i in range(1, t + 1):
                    cc = lsum([a * b for a, b in zip(ld(pt_s, i, g), dmixs[g])])
                    mt_s[tri(t, i), rows(g), :] = cc
                    ms[g].append(cc)
            for g in groups(c, t):
                df = None
                for i in range(1, t + 1):
                    term = [ms[g][i - 1] * p for p in ld(pt_s, i, g)]
                    df = term if df is None else [a + b for a, b in zip(df, term)]
                dps[g - 2 * c] = dmixs[g] if df is None else [a + b * s for a, b, s in zip(dmixs[g], df, ld(slope_s, t, g))]
            db = [jnp.concatenate([dps[0][k], dps[1][k]], 0).astype(BF16) for k in range(NT)]
            for k in range(NT):
                dpre_s[step_rows(c, t), cut(k)] = db[k]
            mm(c, db, True, c == on[-1], True if t > 0 else None)
        for c in on:
            Ss = {}
            if t > 0:
                for g in groups(c, t):
                    S = None
                    for kk in range(ends[g] - 1, t - 1, -1):
                        q = tri(kk, t)
                        dm = ld(dmix_s, kk, g) if kk > t else dmixs[g]
                        f, m = f_s[q, rows(g), :], mt_s[q, rows(g), :]
                        term = [f * a + m * b for a, b in zip(dm, ld(first_s, kk, g))]
                        S = term if S is None else [a + b for a, b in zip(S, term)]
                    Ss[g] = [a * kappa(t) for a in S]
            fr = pop(c)
            gxs[seqs(c, t), :] = pltpu.roll(fr[3], 128 - OFF, 1)
            if t > 0:
                for g in groups(c, t):
                    j = g - 2 * c
                    for k in range(NT):
                        v = fr[k][j * SUB:(j + 1) * SUB, :] + Ss[g][k]
                        grad_s[rows(g), cut(k)] = v if t < LEAST else jnp.where(live(g, t), v, tots[g][k])
        for k in range(NT):
            sums_out[:SUB, cut(k)] += sums[0][k]
            sums_out[SUB:, cut(k)] += sums[1][k]

    todo = list(range(B))
    for t in range(TV):
        fwd_step(t)
        n = -(-len(todo) // (TV - t))
        for r in todo[:n]:
            sort_cot(r)
        todo = todo[n:]
    todo = list(range(B // 2))
    for t in range(TV - 1, -1, -1):
        bwd_step(t)
        n = -(-len(todo) // (t + 1))
        for i in todo[:n]:
            fin(i)
        todo = todo[n:]
    for t in range(TV, T):
        gxs[pl.ds(t, B, stride=T), :] = jnp.zeros((B, 128), F32)


def cell_call(info, xs, lens, cotf, wc, gain_p, shift_p):
    V = pltpu.VMEM
    S = jax.ShapeDtypeStruct
    big = V((TV, B, HP), F32)
    pair = V((NP, B, 128), F32)
    seq, wide = V((B * T, 128), F32), V((NT, B * T, 128), F32)
    vs = pl.BlockSpec(memory_space=pltpu.VMEM)
    return pl.pallas_call(
        cell_body,
        out_shape=(S((B * T, H), BF16), S((B * T, E), F32), S((TV * B, HP), BF16), S((TV * B, HP), BF16), S((2 * SUB, HP), F32)),
        in_specs=[pl.BlockSpec(memory_space=pltpu.SMEM)] + [vs] * 6,
        scratch_shapes=[seq, wide, seq, wide, V((B, HP), F32), V((B, HP), F32),
            big, big, big, big, V((TV, B, 128), F32), big, big, pair, pair, big],
        compiler_params=pltpu.CompilerParams(vmem_limit_bytes=44 * 2**20),
    )(info, xs, lens, cotf, wc, gain_p, shift_p)


MESH = pl.DeviceIdType.MESH
PR = 416
XR = 104
Q = 4
QC = E // Q


def pack(main, extra, lane_of):
    pieces = []
    for q in range(Q):
        m = main(q)
        x = pltpu.roll(extra, E - QC * q, 1) if E != QC * q else extra
        pieces.append(jnp.where(lane_of < E, m, jnp.where(lane_of < E + QC, x, 0.0)))
    return pieces


def unpack_extra(block, lane_of):
    out = None
    for q in range(Q):
        x = pltpu.roll(block(q), 128 - E + QC * q, 1)
        keep = (lane_of >= QC * q) & (lane_of < QC * (q + 1))
        out = jnp.where(keep, x, 0.0 if out is None else out)
    return out


def gather_body(w_ref, c_ref, bias_ref, len_ref, x_ref, cot_ref, gain_ref, shift_ref,
        wc_out, info_out, lens_out, xs_out, cotf_out, gain_out, shift_out,
        w_v, c_v, bias_v, len_v, x_v, cot_v, gain_v, shift_v, blk, stage, cst, brow, xpad, ssem, rsem, lsem):
    me, b = lax.axis_index("tm"), lax.axis_index("batch")
    sib, xp, diag = lax.bitwise_xor(me, 1), lax.bitwise_xor(me, 2), lax.bitwise_xor(me, 3)
    barrier = pltpu.get_barrier_semaphore()
    for peer in (xp, diag, sib):
        pl.semaphore_signal(barrier, inc=1, device_id=(peer, b), device_id_type=MESH)
    pairs = ((w_ref, w_v), (c_ref, c_v), (x_ref, x_v), (cot_ref, cot_v), (bias_ref, bias_v), (len_ref, len_v), (gain_ref, gain_v), (shift_ref, shift_v))
    loads = [pltpu.make_async_copy(s, d, lsem.at[n]) for n, (s, d) in enumerate(pairs)]
    for cp in loads:
        cp.start()
    lane = lax.broadcasted_iota(jnp.int32, (XR, 128), 1)
    stage[...] = jnp.zeros((PR, 128), F32)
    cst[...] = jnp.zeros((XR, 128), F32)
    loads[0].wait()
    loads[1].wait()
    stage[:H, :E] = w_v[...].astype(F32)
    cst[:E, :E] = c_v[...].astype(F32)
    for q, p in enumerate(pack(lambda q: stage[q * XR:(q + 1) * XR, :], cst[...], lane)):
        stage[q * XR:(q + 1) * XR, :] = p
    blk[me] = stage[...].astype(BF16)
    pl.semaphore_wait(barrier, 3)
    cuts = ((0, 128), (128, 128), (256, PR - 256))
    def copy(n, slot, r0, nr, peer):
        return pltpu.make_async_remote_copy(src_ref=blk.at[slot, pl.ds(r0, nr)], dst_ref=blk.at[slot, pl.ds(r0, nr)],
            send_sem=ssem.at[n], recv_sem=rsem.at[n], device_id=(peer, b), device_id_type=MESH)
    first = [copy(n, me, r0, nr, xp) for n, (r0, nr) in enumerate(cuts)]
    first.append(copy(3, me, *cuts[2], diag))
    first.append(copy(4, me, 0, PR, sib))
    for cp in first:
        cp.start()
    for cp in loads[2:]:
        cp.wait()
    xpad[...] = jnp.zeros((48, 128), F32)
    def prep(i, _):
        r = pl.ds(pl.multiple_of(i * 48, 48), 48)
        l = lax.broadcasted_iota(jnp.int32, (48, 128), 1)
        xpad[:, :E] = x_v[r, :].astype(F32)
        xs_out[r, :] = jnp.where(l < OFF + E, pltpu.roll(xpad[...], OFF, 1), jnp.where(l < OFF + E + ONES, 1.0, 0.0))
        for k in range(3):
            cotf_out[k, r, :] = cot_v[r, k * 128:(k + 1) * 128].astype(F32)
        cotf_out[3, r, :] = jnp.zeros((48, 128), F32)
        cotf_out[3, r, :OFF] = cot_v[r, LT:].astype(F32)
        return 0
    lax.fori_loop(0, B * T // 48, prep, 0)
    col48 = lax.broadcasted_iota(jnp.int32, (B, B), 1)
    row48 = lax.broadcasted_iota(jnp.int32, (B, B), 0)
    def turn(col):
        return jnp.sum(jnp.where(col48 == row48, jnp.broadcast_to(col, (B, B)), 0.0), 0, keepdims=True)
    ln = jnp.broadcast_to(len_v[...], (B, B)).astype(F32)
    key = ln * 64.0 + (B - 1 - col48).astype(F32)
    kcol = jnp.sum(jnp.where(col48 == row48, key, 0.0), 1, keepdims=True)
    rank = jnp.sum(jnp.where(kcol > key, 1.0, 0.0), 0, keepdims=True)
    hit = jnp.broadcast_to(rank, (B, B)) == row48.astype(F32)
    lcol = jnp.sum(jnp.where(hit, ln, 0.0), 1, keepdims=True)
    lens_out[...] = jnp.broadcast_to(lcol, (B, 128))
    most = jnp.zeros((B, 1), F32)
    row1 = lax.broadcasted_iota(jnp.int32, (B, 1), 0)
    for g, end in enumerate(PLANS[0]):
        most = jnp.where(row1 // SUB == g, float(end), most)
    fits = jnp.where(jnp.max(lcol - most, 0, keepdims=True) > 0.0, 0.0, 1.0)
    info_out[...] = jnp.zeros((SUB, 128), jnp.int32)
    info_out[0:1, :B] = rank.astype(jnp.int32)
    info_out[1:2, :B] = turn(jnp.sum(jnp.where(hit, col48.astype(F32), 0.0), 1, keepdims=True)).astype(jnp.int32)
    info_out[2:3, :B] = jnp.broadcast_to(fits, (1, B)).astype(jnp.int32)
    for src, out in ((gain_v, gain_out), (shift_v, shift_out)):
        out[...] = jnp.zeros((SUB, HP), F32)
        out[:, :H] = jnp.broadcast_to(src[...], (SUB, H))
    brow[...] = jnp.zeros((SUB, HP), F32)
    brow[:1, :H] = bias_v[...]
    passed = []
    for n in range(2):
        first[n].wait_recv()
        cp = copy(5 + n, xp, *cuts[n], sib)
        cp.start()
        passed.append(cp)
    for cp in first[2:] + passed:
        cp.wait_recv()
    for cp in first + passed:
        cp.wait_send()
    bias = brow[:1, :]
    hi = bias.astype(BF16).astype(F32)
    mid = (bias - hi).astype(BF16).astype(F32)
    lo = bias - hi - mid
    def lay(rows, l):
        b0, b1, b2, b3 = rows
        b1, b2, b3 = pltpu.roll(b1, 100, 1), pltpu.roll(b2, 72, 1), pltpu.roll(b3, 44, 1)
        return [jnp.where(l < 100, b0, b1), jnp.where(l < 72, b1, b2), jnp.where(l < 44, b2, b3), jnp.where(l < 16, b3, 0.0)]
    l80 = lax.broadcasted_iota(jnp.int32, (80, 128), 1)
    for r in range(0, H, 80):
        for k, v in enumerate(lay([blk[k, r:r + 80, :].astype(F32) for k in range(4)], l80)):
            wc_out[r:r + 80, k * 128:(k + 1) * 128] = v.astype(BF16)
    for k in range(4):
        stage[...] = blk[k].astype(F32)
        cst4 = unpack_extra(lambda q: stage[q * XR:(q + 1) * XR, :], lane)
        blk[k, :XR + 8, :] = jnp.concatenate([cst4, jnp.zeros((8, 128), F32)], 0).astype(BF16)
    row = lax.broadcasted_iota(jnp.int32, (HP - H, 128), 0)
    l112 = lax.broadcasted_iota(jnp.int32, (HP - H, 128), 1)
    for k, v in enumerate(lay([blk[k, :HP - H, :].astype(F32) for k in range(4)], l112)):
        for n, part in enumerate((hi, mid, lo)):
            v = jnp.where(row == E + n, jnp.broadcast_to(part[:, k * 128:(k + 1) * 128], (HP - H, 128)), v)
        wc_out[H:, k * 128:(k + 1) * 128] = v.astype(BF16)


def gather_call(w, c, bias, lengths, x, cot, gain, shift):
    D = pltpu.SemaphoreType.DMA
    V = pltpu.VMEM
    S = jax.ShapeDtypeStruct
    return pl.pallas_call(
        gather_body,
        out_shape=(S((HP, HP), BF16), S((SUB, 128), jnp.int32), S((B, 128), F32), S((B * T, 128), F32), S((NT, B * T, 128), F32), S((SUB, HP), F32), S((SUB, HP), F32)),
        in_specs=[pl.BlockSpec(memory_space=pltpu.HBM)] * 8,
        scratch_shapes=[V((H, E), BF16), V((E, E), BF16), V((1, H), F32), V((1, B), jnp.int32), V((B * T, E), BF16), V((B * T, H), BF16),
            V((1, H), F32), V((1, H), F32),
            V((4, PR, 128), BF16), V((PR, 128), F32), V((XR, 128), F32), V((SUB, HP), F32), V((48, 128), F32), D((7,)), D((7,)), D((8,))],
        compiler_params=pltpu.CompilerParams(collective_id=0, has_side_effects=True, vmem_limit_bytes=12 * 2**20),
    )(*[pltpu.with_memory_space_constraint(v, pltpu.HBM) for v in (
        w, c, bias.reshape(1, H), lengths.reshape(1, B), x.reshape(B * T, E), cot.reshape(B * T, H), gain.reshape(1, H), shift.reshape(1, H))])


OWN = 4
FIRST = 2


def spans():
    tiles = PR // 16
    return tiles // OWN, tiles % OWN


def reduce_body(nb, hx, dp, sums_ref, out_ref, blk, pk, sib_in, rs_out, rs_in, ssem, srsem, rsem_s, rsem_r, asem_s, asem_r):
    me, b = lax.axis_index("tm"), lax.axis_index("batch")
    core, sib, xi = lax.rem(me, 2), lax.bitwise_xor(me, 1), me // 2
    group = b // nb * nb
    rank = b - group
    base, more = spans()
    big, small = (base + 1) * 16, base * 16
    barrier = pltpu.get_barrier_semaphore()
    pl.semaphore_signal(barrier, inc=1, device_id=(sib, b), device_id_type=MESH)
    others = [(dx, db) for db in range(nb) for dx in range(2) if dx or db]
    for dx, db in others:
        pl.semaphore_signal(barrier, inc=1, device_id=(2 * lax.rem(xi + dx, 2) + core, group + lax.rem(rank + db, nb)), device_id_type=MESH)
    def blocks(t, l):
        t0, t1, t2, t3 = t
        return [t0,
            jnp.where(l < 28, pltpu.roll(t0, 28, 1), pltpu.roll(t1, 28, 1)),
            jnp.where(l < 56, pltpu.roll(t1, 56, 1), pltpu.roll(t2, 56, 1)),
            jnp.where(l < 84, pltpu.roll(t2, 84, 1), pltpu.roll(t3, 84, 1))]
    gsum = jnp.sum(sums_ref[:SUB, :], 0, keepdims=True)
    ssum = jnp.sum(sums_ref[SUB:, :], 0, keepdims=True)
    l128 = lax.broadcasted_iota(jnp.int32, (128, 128), 1)
    r128 = lax.broadcasted_iota(jnp.int32, (128, 128), 0)
    for m in range(4):
        prod = lax.dot_general(hx[:, m * 128:(m + 1) * 128], dp[...], (((0,), (0,)), ((), ())), preferred_element_type=F32)
        t = [prod[:, k * 128:(k + 1) * 128] for k in range(4)]
        if m == 3:
            for k in range(4):
                gk = jnp.broadcast_to(gsum[:, k * 128:(k + 1) * 128], (128, 128))
                sk = jnp.broadcast_to(ssum[:, k * 128:(k + 1) * 128], (128, 128))
                t[k] = jnp.where(r128 == OFF + E + 1, gk, jnp.where(r128 == OFF + E + 2, sk, t[k]))
        for k, v in enumerate(blocks(t, l128)):
            blk[k, m * 128:(m + 1) * 128, :] = v
    lane = lax.broadcasted_iota(jnp.int32, (XR, 128), 1)
    for k in range(4):
        extra = blk[k, H:H + XR, :]
        blk[k, H:H + 16, :] = jnp.zeros((16, 128), F32)
        for q, p in enumerate(pack(lambda q: blk[k, q * XR:(q + 1) * XR, :], extra, lane)):
            blk[k, q * XR:(q + 1) * XR, :] = p
        pk[k] = blk[k, :PR, :].astype(BF16)
    pl.semaphore_wait(barrier, len(others) + 1)
    scopies = []
    for j in range(2):
        cp = pltpu.make_async_remote_copy(src_ref=pk.at[2 * j + (1 - core)], dst_ref=sib_in.at[j], send_sem=ssem.at[j], recv_sem=srsem.at[j],
            device_id=(sib, b), device_id_type=MESH)
        cp.start()
        scopies.append(cp)
    def sized(owner, run):
        pl.when(owner < more)(lambda: run(big))
        pl.when(owner >= more)(lambda: run(small))
    def span(owner, rows):
        return pl.ds(pl.multiple_of((owner * base + lax.min(owner, more)) * 16, 16), rows)
    mine = xi * nb + rank
    owner = rank - FIRST
    is_owner = (owner >= 0) & (owner < OWN)
    far = 2 - 2 * (rank // (nb // 2))
    def rcopy(px, o, rows):
        n = px * OWN + o
        return pltpu.make_async_remote_copy(src_ref=rs_out.at[px, span(o, rows)], dst_ref=rs_in.at[mine, pl.ds(0, rows)],
            send_sem=rsem_s.at[n], recv_sem=rsem_r.at[mine], device_id=(2 * px + core, group + FIRST + o), device_id_type=MESH)
    def arrived(slot, rows):
        return pltpu.make_async_remote_copy(src_ref=rs_out.at[0, pl.ds(0, rows)], dst_ref=rs_in.at[slot, pl.ds(0, rows)],
            send_sem=rsem_s.at[0], recv_sem=rsem_r.at[slot], device_id=(2 * (1 - xi) + core, b), device_id_type=MESH)
    def targets():
        for px in range(2):
            for n in range(OWN):
                o = lax.rem(far + n, OWN)
                yield px, o, (px != xi) | (o != owner)
    def acopy(db, o, rows):
        return pltpu.make_async_remote_copy(src_ref=out_ref.at[span(o, rows)], dst_ref=out_ref.at[span(o, rows)], send_sem=asem_s.at[db],
            recv_sem=asem_r.at[o], device_id=(me, group + lax.rem(rank + db, nb)), device_id_type=MESH)
    for j in range(2):
        scopies[j].wait_recv()
        rs_out[j] = (blk[2 * j + core, :PR, :] + sib_in[j].astype(F32)).astype(BF16)
        for px, o, other in targets():
            if px == j:
                pl.when(other)(lambda px=px, o=o: sized(o, lambda rows: rcopy(px, o, rows).start()))
    def collect(rows):
        total = rs_out[xi, span(owner, rows), :].astype(F32)
        for n in range(1, 2 * nb):
            slot = lax.rem(mine + n, 2 * nb)
            arrived(slot, rows).wait_recv()
            total = total + rs_in[slot, :rows, :].astype(F32)
        out_ref[span(owner, rows), :] = total.astype(BF16)
        for db in range(1, nb):
            acopy(db, owner, rows).start()
    pl.when(is_owner)(lambda: sized(owner, collect))
    for o in range(OWN):
        rows = big if o < more else small
        pl.when(owner != o)(lambda o=o, rows=rows: acopy(1, o, rows).wait_recv())
    for cp in scopies:
        cp.wait_send()
    for px, o, other in targets():
        pl.when(other)(lambda px=px, o=o: sized(o, lambda rows: rcopy(px, o, rows).wait_send()))
    def sent(rows):
        for db in range(1, nb):
            acopy(db, owner, rows).wait_send()
    pl.when(is_owner)(lambda: sized(owner, sent))


def reduce_call(hx, dp, sums, nb):
    D = pltpu.SemaphoreType.DMA
    V = pltpu.VMEM
    vs = pl.BlockSpec(memory_space=pltpu.VMEM)
    big = (spans()[0] + 1) * 16
    return pl.pallas_call(
        functools.partial(reduce_body, nb),
        out_shape=jax.ShapeDtypeStruct((PR, 128), BF16),
        in_specs=[vs, vs, vs],
        out_specs=vs,
        scratch_shapes=[V((4, HP, 128), F32), V((4, PR, 128), BF16), V((2, PR, 128), BF16),
            V((2, PR, 128), BF16), V((2 * nb, big, 128), BF16),
            D((2,)), D((2,)), D((2 * OWN,)), D((2 * nb,)), D((nb,)), D((OWN,))],
        compiler_params=pltpu.CompilerParams(collective_id=1, has_side_effects=True, vmem_limit_bytes=16 * 2**20),
    )(hx, dp, sums)


def spread_body(p_ref, gw_out, gc_out, gb_out, gg_out, gs_out, stage):
    stage[...] = p_ref[...].astype(F32)
    gw_out[...] = stage[:H, :E]
    lane = lax.broadcasted_iota(jnp.int32, (XR, 128), 1)
    extra = unpack_extra(lambda q: stage[q * XR:(q + 1) * XR, :], lane)
    stage[:XR, :] = extra
    gc_out[...] = stage[:E, :E]
    for n, ref in enumerate((gb_out, gg_out, gs_out)):
        ref[...] = stage[E + n:E + n + 1, :E]


def spread_call(p):
    S = jax.ShapeDtypeStruct
    vec = S((1, E), F32)
    return pl.pallas_call(
        spread_body,
        out_shape=(S((H, E), F32), S((E, E), F32), vec, vec, vec),
        scratch_shapes=[pltpu.VMEM((PR, 128), F32)],
        compiler_params=pltpu.CompilerParams(vmem_limit_bytes=8 * 2**20),
    )(p)


def per_device(inputs, lengths, w_rec, w_in, rec_bias, norm_gain, norm_shift, cotangent, nb):
    wc, info, lens, xs, cotf, gain, shift = gather_call(w_rec, w_in, rec_bias, lengths, inputs, cotangent, norm_gain, norm_shift)
    hid, gx, hx, dp, sums = cell_call(info, xs, lens, cotf, wc, gain, shift)
    group = math.gcd(nb, 8)
    p = reduce_call(hx, dp, sums, group)
    if nb > group:
        p = lax.all_gather(p.astype(F32), "batch").reshape(nb // group, group, PR, 128)[:, 0].sum(0)
    gw, gc, gb, gg, gs = spread_call(p)
    return hid.reshape(B, T, H), gx.reshape(B, T, E), gw, gc, gb.reshape(E), gg.reshape(E), gs.reshape(E)


def solution(mesh):
    both = ("tm", "batch")
    return jax.shard_map(
        functools.partial(per_device, nb=mesh.shape["batch"]),
        mesh=mesh,
        in_specs=(P(both, None, None), P(both), P(None, "tm"), P(None, "tm"), P(), P(), P(), P(both, None, None)),
        out_specs=(P(both, None, None), P(both, None, None), P(None, "tm"), P(None, "tm"), P("tm"), P("tm"), P("tm")),
        check_vma=False,
    )
```

```python
import functools, math
import jax, jax.numpy as jnp
from jax import lax
from jax.experimental import pallas as pl
from jax.experimental.pallas import tpu as pltpu
from jax.sharding import PartitionSpec as P
F32, BF16 = jnp.float32, jnp.bfloat16
DECAY, RATE, EPS = 0.95, 0.5, 1e-5
B, T, TV, H, E = 48, 24, 21, 400, 100
HP = 512
NT = 4
LT = H // 128 * 128
OFF = H - LT
SUB = 8
ROWS = 16
NC = B // ROWS
NP = TV * (TV - 1) // 2
ONES = 3
LEAST = 5

def kappa(i):
    return math.sqrt(RATE) * DECAY ** (-i / 2)

def tri(t, i):
    return t * (t - 1) // 2 + i - 1

PLANS = ((21, 21, 19, 17, 14, 11), (TV,) * (B // SUB))


def cell_body(info, xs_in, lens_ref, cotf_in, wc_ref, gain_p, shift_p, hid_out, gx_out, hx, dpre_s, sums_out, hid_v, sem, xs, cotf, gxs, hidf, h_s, *rest):
    accs = [pltpu.ACC(m)((ROWS, 256), F32) for _ in range(NC) for m in range(2)]
    def place(row, n):
        return pl.ds(pl.multiple_of(info[row, n] * T, SUB), T)
    for r in range(B):
        xs[r * T:(r + 1) * T, :] = xs_in[place(1, r), :]
    hid_copy = pltpu.make_async_copy(hid_v, hid_out, sem)
    h_s[...] = jnp.zeros((B, HP), F32)
    sums_out[...] = jnp.zeros((2 * SUB, HP), F32)
    def scoped(*a):
        def run(ends):
            cell_inner(info[2, 0] >= 0, ends, place, xs, lens_ref, cotf_in, wc_ref, gain_p, shift_p, hid_v, hx, dpre_s, sums_out, hid_copy,
                cotf, gxs, hidf, h_s, *rest, [a[2 * i:2 * i + 2] for i in range(NC)])
        lax.cond(info[2, 0] > 0, lambda: run(PLANS[0]), lambda: run(PLANS[1]))
    pl.run_scoped(scoped, *accs)
    for b in range(B):
        gx_out[b * T:(b + 1) * T, :] = gxs[place(0, b), :E]
    hid_copy.wait()


def cell_inner(go, ends, place, xs, lens_ref, cotf_in, wc_ref, gain_p, shift_p, hid_out, hx, dpre_s, sums_out, hid_copy,
        cotf, gxs, hidf, h_s, grad_s, first_s, slope_s, s_s, xh_s, rstd_s, pt_s, pc_s, f_s, mt_s, dmix_s, accs):
    lane = lax.broadcasted_iota(jnp.int32, (SUB, 128), 1)
    lane16 = lax.broadcasted_iota(jnp.int32, (ROWS, 128), 1)
    tail = lane < OFF
    zero = jnp.zeros((SUB, 128), F32)
    zb = jnp.zeros((ROWS, HP), BF16)
    def chains(t): return [c for c in range(NC) if ends[2 * c] > t]
    def groups(c, t): return [g for g in (2 * c, 2 * c + 1) if ends[g] > t]
    def rows(g): return slice(g * SUB, (g + 1) * SUB)
    def crow(c): return slice(c * ROWS, (c + 1) * ROWS)
    def cut(k): return slice(k * 128, (k + 1) * 128)
    def ld(ref, t, g): return [ref[t, rows(g), cut(k)] for k in range(NT)]
    def st(ref, t, g, v):
        for k in range(NT):
            ref[t, rows(g), cut(k)] = v[k]
    def lsum(v):
        return jnp.broadcast_to(jnp.sum((v[0] + v[1]) + (v[2] + v[3]), -1, keepdims=True), (SUB, 128))
    def only_h(v): return [v[0], v[1], v[2], jnp.where(tail, v[3], 0.0)]
    def push(k, transpose):
        for m in range(2):
            if transpose:
                w = wc_ref[m * 256:(m + 1) * 256, k * 256:(k + 1) * 256]
            else:
                w = wc_ref[k * 256:(k + 1) * 256, m * 256:(m + 1) * 256]
            pltpu.matmul_push_rhs(w, k, m, transpose=transpose)
    def mm(c, v, transpose, last, after):
        lhs = [jnp.concatenate(v[:2], 1), jnp.concatenate(v[2:], 1)]
        o = (0, 1) if c % 2 == 0 else (1, 0)
        for n, k in enumerate(o):
            for m in range(2):
                pltpu.matmul_acc_lhs(accs[c][m], lhs[k], load_staged_rhs=k if n or c == 0 else None)
            if n == 0 and c > 0:
                push(o[1], transpose)
        if last and after is not None:
            push(0, after), push(1, after)
    def pop(c):
        u = [pltpu.matmul_pop(accs[c][m]) for m in range(2)]
        return [u[0][:, :128], u[0][:, 128:], u[1][:, :128], u[1][:, 128:]]
    push(0, False), push(1, False)
    def sort_cot(r):
        for k in range(NT):
            cotf[k, r * T:(r + 1) * T, :] = cotf_in[k, place(1, r), :]
    def fin(i):
        r = slice(i * 2 * T, (i + 1) * 2 * T)
        for k in range(NT):
            v = jnp.concatenate([hidf[k, place(0, 2 * i + j), :] for j in range(2)], 0).astype(BF16)
            hid_out[r, k * 128:min((k + 1) * 128, H)] = v[:, :min(128, H - k * 128)]
    def live(g, t):
        return lens_ref[rows(g), :] > t
    def seqs(c, t): return pl.ds(c * ROWS * T + t, ROWS, stride=T)
    def gseqs(g, t): return pl.ds(g * SUB * T + t, SUB, stride=T)
    def step_rows(c, t): return slice(t * B + c * ROWS, t * B + (c + 1) * ROWS)

    def fwd_step(t):
        dec = DECAY ** t
        on = chains(t)
        for c in range(NC):
            if c not in on:
                hx[step_rows(c, t), :] = zb
                continue
            hv = [h_s[crow(c), cut(k)] for k in range(NT)]
            hv[3] = jnp.where(lane16 < OFF, hv[3], xs[seqs(c, t), :])
            hb = [v.astype(BF16) for v in hv]
            for k in range(NT):
                hx[step_rows(c, t), cut(k)] = hb[k]
            mm(c, hb, False, c == on[-1], t == TV - 1)
        if t > 0:
            for c in on:
                for g in groups(c, t):
                    pt = [h_s[rows(g), cut(k)] * kappa(t) for k in range(NT)]
                    st(pt_s, t, g, pt)
                    mp = lsum(pt) * (1.0 / H)
                    st(pc_s, t, g, only_h([v - mp for v in pt]))
        for c in on:
            u16 = pop(c)
            cs, us = {}, {}
            for g in groups(c, t):
                j = g - 2 * c
                u = [v[j * SUB:(j + 1) * SUB, :] for v in u16]
                mu = lsum(u) * (1.0 / H)
                us[g] = only_h([v - mu for v in u])
                sg = [jax.nn.sigmoid(v) for v in u]
                sgd = [v * dec for v in sg]
                first = [a * b for a, b in zip(u, sgd)]
                st(first_s, t, g, first)
                st(slope_s, t, g, [a + f - f * s for a, f, s in zip(sgd, first, sg)])
                cs[g] = []
                for i in range(1, t + 1):
                    cc = lsum([a * b for a, b in zip(ld(pt_s, i, g), first)])
                    f_s[tri(t, i), rows(g), :] = cc
                    cs[g].append(cc)
            for g in groups(c, t):
                mc = us[g]
                for i in range(1, t + 1):
                    mc = [m + cs[g][i - 1] * p for m, p in zip(mc, ld(pc_s, i, g))]
                var = lsum([m * m for m in mc]) * (1.0 / H)
                rstd = lax.rsqrt(var + EPS)
                xh = [m * rstd for m in mc]
                z = [x * gain_p[:, cut(k)] + shift_p[:, cut(k)] for k, x in enumerate(xh)]
                sz = [jax.nn.sigmoid(v) for v in z]
                out = [a * b for a, b in zip(z, sz)]
                new = out
                if t >= LEAST:
                    ok = live(g, t)
                    new = [jnp.where(ok, a, h_s[rows(g), cut(k)]) for k, a in enumerate(out)]
                for k in range(NT):
                    h_s[rows(g), cut(k)] = new[k]
                    for tt in [t] if t < ends[g] - 1 else range(t, T):
                        hidf[k, gseqs(g, tt), :] = new[k]
                st(xh_s, t, g, xh)
                rstd_s[t, rows(g), :] = rstd
                st(s_s, t, g, [a + o - o * a for a, o in zip(sz, out)])

    def bwd_step(t):
        on = chains(t)
        sums = [None, None]
        dmixs, tots, ms = {}, {}, {}
        for c in range(NC):
            if c not in on:
                dpre_s[step_rows(c, t), :] = zb
                gxs[seqs(c, t), :] = jnp.zeros((ROWS, 128), F32)
                continue
            dps = [[zero] * NT, [zero] * NT]
            for g in groups(c, t):
                if t == ends[g] - 1:
                    tot = [cotf[k, gseqs(g, T - 1), :] for k in range(NT)]
                    for tt in range(T - 2, t - 1, -1):
                        tot = [a + cotf[k, gseqs(g, tt), :] for k, a in enumerate(tot)]
                else:
                    tot = [grad_s[rows(g), cut(k)] + cotf[k, gseqs(g, t), :] for k in range(NT)]
                tots[g] = tot
                xh = ld(xh_s, t, g)
                d = tot if t < LEAST else [jnp.where(live(g, t), a, 0.0) for a in tot]
                dz = [a * s for a, s in zip(d, ld(s_s, t, g))]
                gs = [a * b for a, b in zip(dz, xh)]
                sums = [gs, dz] if sums[0] is None else [[a + b for a, b in zip(p, q)] for p, q in zip(sums, (gs, dz))]
                dxh = [a * gain_p[:, cut(k)] for k, a in enumerate(dz)]
                m1 = lsum(dxh) * (1.0 / H)
                m2 = lsum([a * b for a, b in zip(dxh, xh)]) * (1.0 / H)
                rstd = rstd_s[t, rows(g), :]
                dmixs[g] = only_h([rstd * (a - m1 - b * m2) for a, b in zip(dxh, xh)])
                st(dmix_s, t, g, dmixs[g])
            for g in groups(c, t):
                ms[g] = []
                for i in range(1, t + 1):
                    cc = lsum([a * b for a, b in zip(ld(pt_s, i, g), dmixs[g])])
                    mt_s[tri(t, i), rows(g), :] = cc
                    ms[g].append(cc)
            for g in groups(c, t):
                df = None
                for i in range(1, t + 1):
                    term = [ms[g][i - 1] * p for p in ld(pt_s, i, g)]
                    df = term if df is None else [a + b for a, b in zip(df, term)]
                dps[g - 2 * c] = dmixs[g] if df is None else [a + b * s for a, b, s in zip(dmixs[g], df, ld(slope_s, t, g))]
            db = [jnp.concatenate([dps[0][k], dps[1][k]], 0).astype(BF16) for k in range(NT)]
            for k in range(NT):
                dpre_s[step_rows(c, t), cut(k)] = db[k]
            mm(c, db, True, c == on[-1], True if t > 0 else None)
        for c in on:
            Ss = {}
            if t > 0:
                for g in groups(c, t):
                    S = None
                    for kk in range(ends[g] - 1, t - 1, -1):
                        q = tri(kk, t)
                        dm = ld(dmix_s, kk, g) if kk > t else dmixs[g]
                        f, m = f_s[q, rows(g), :], mt_s[q, rows(g), :]
                        term = [f * a + m * b for a, b in zip(dm, ld(first_s, kk, g))]
                        S = term if S is None else [a + b for a, b in zip(S, term)]
                    Ss[g] = [a * kappa(t) for a in S]
            fr = pop(c)
            gxs[seqs(c, t), :] = pltpu.roll(fr[3], 128 - OFF, 1)
            if t > 0:
                for g in groups(c, t):
                    j = g - 2 * c
                    for k in range(NT):
                        v = fr[k][j * SUB:(j + 1) * SUB, :] + Ss[g][k]
                        grad_s[rows(g), cut(k)] = v if t < LEAST else jnp.where(live(g, t), v, tots[g][k])
        for k in range(NT):
            sums_out[:SUB, cut(k)] += sums[0][k]
            sums_out[SUB:, cut(k)] += sums[1][k]

    def fwd_part(t):
        fwd_step(t)
        for r in range(-(-B * t // TV), -(-B * (t + 1) // TV)):
            sort_cot(r)
    def bwd_part(t):
        bwd_step(t)
        for i in range(2 * (TV - 1 - t), min(2 * (TV - t), B // 2)):
            fin(i)
    for t in range(TV):
        pl.when(go)(lambda t=t: fwd_part(t))
    for t in range(TV - 1, -1, -1):
        pl.when(go)(lambda t=t: bwd_part(t))
        if t == TV - B // 4:
            hid_copy.start()
    for t in range(TV, T):
        gxs[pl.ds(t, B, stride=T), :] = jnp.zeros((B, 128), F32)


def cell_call(info, xs, lens, cotf, wc, gain_p, shift_p):
    V = pltpu.VMEM
    S = jax.ShapeDtypeStruct
    big = V((TV, B, HP), F32)
    pair = V((NP, B, 128), F32)
    seq, wide = V((B * T, 128), F32), V((NT, B * T, 128), F32)
    vs = pl.BlockSpec(memory_space=pltpu.VMEM)
    return pl.pallas_call(
        cell_body,
        out_specs=[pl.BlockSpec(memory_space=pl.ANY)] + [vs] * 4,
        out_shape=(S((B * T, H), BF16), S((B * T, E), F32), S((TV * B, HP), BF16), S((TV * B, HP), BF16), S((2 * SUB, HP), F32)),
        in_specs=[pl.BlockSpec(memory_space=pltpu.SMEM)] + [vs] * 6,
        scratch_shapes=[V((B * T, H), BF16), pltpu.SemaphoreType.DMA, seq, wide, seq, wide, V((B, HP), F32), V((B, HP), F32),
            big, big, big, big, V((TV, B, 128), F32), big, big, pair, pair, big],
        compiler_params=pltpu.CompilerParams(vmem_limit_bytes=44 * 2**20),
    )(info, xs, lens, cotf, wc, gain_p, shift_p)


MESH = pl.DeviceIdType.MESH
PR = 416
XR = 104
Q = 4
QC = E // Q


def pack(main, extra, lane_of):
    pieces = []
    for q in range(Q):
        m = main(q)
        x = pltpu.roll(extra, E - QC * q, 1) if E != QC * q else extra
        pieces.append(jnp.where(lane_of < E, m, jnp.where(lane_of < E + QC, x, 0.0)))
    return pieces


def unpack_extra(block, lane_of):
    out = None
    for q in range(Q):
        x = pltpu.roll(block(q), 128 - E + QC * q, 1)
        keep = (lane_of >= QC * q) & (lane_of < QC * (q + 1))
        out = jnp.where(keep, x, 0.0 if out is None else out)
    return out


def gather_body(w_ref, c_ref, bias_ref, len_ref, x_ref, cot_ref, gain_ref, shift_ref,
        wc_out, info_out, lens_out, xs_out, cotf_out, gain_out, shift_out,
        w_v, c_v, bias_v, len_v, x_v, cot_v, gain_v, shift_v, blk, stage, cst, brow, xpad, ssem, rsem, lsem):
    me, b = lax.axis_index("tm"), lax.axis_index("batch")
    sib, xp, diag = lax.bitwise_xor(me, 1), lax.bitwise_xor(me, 2), lax.bitwise_xor(me, 3)
    barrier = pltpu.get_barrier_semaphore()
    for peer in (xp, diag, sib):
        pl.semaphore_signal(barrier, inc=1, device_id=(peer, b), device_id_type=MESH)
    pairs = ((w_ref, w_v), (c_ref, c_v), (x_ref, x_v), (cot_ref, cot_v), (bias_ref, bias_v), (len_ref, len_v), (gain_ref, gain_v), (shift_ref, shift_v))
    loads = [pltpu.make_async_copy(s, d, lsem.at[n]) for n, (s, d) in enumerate(pairs)]
    for cp in loads:
        cp.start()
    lane = lax.broadcasted_iota(jnp.int32, (XR, 128), 1)
    stage[...] = jnp.zeros((PR, 128), F32)
    cst[...] = jnp.zeros((XR, 128), F32)
    loads[0].wait()
    loads[1].wait()
    stage[:H, :E] = w_v[...].astype(F32)
    cst[:E, :E] = c_v[...].astype(F32)
    for q, p in enumerate(pack(lambda q: stage[q * XR:(q + 1) * XR, :], cst[...], lane)):
        stage[q * XR:(q + 1) * XR, :] = p
    blk[me] = stage[...].astype(BF16)
    pl.semaphore_wait(barrier, 3)
    cuts = ((0, 128), (128, 128), (256, PR - 256))
    def copy(n, slot, r0, nr, peer):
        return pltpu.make_async_remote_copy(src_ref=blk.at[slot, pl.ds(r0, nr)], dst_ref=blk.at[slot, pl.ds(r0, nr)],
            send_sem=ssem.at[n], recv_sem=rsem.at[n], device_id=(peer, b), device_id_type=MESH)
    first = [copy(n, me, r0, nr, xp) for n, (r0, nr) in enumerate(cuts)]
    first.append(copy(3, me, *cuts[2], diag))
    first.append(copy(4, me, 0, PR, sib))
    for cp in first:
        cp.start()
    for cp in loads[2:]:
        cp.wait()
    xpad[...] = jnp.zeros((48, 128), F32)
    def prep(i, _):
        r = pl.ds(pl.multiple_of(i * 48, 48), 48)
        l = lax.broadcasted_iota(jnp.int32, (48, 128), 1)
        xpad[:, :E] = x_v[r, :].astype(F32)
        xs_out[r, :] = jnp.where(l < OFF + E, pltpu.roll(xpad[...], OFF, 1), jnp.where(l < OFF + E + ONES, 1.0, 0.0))
        for k in range(3):
            cotf_out[k, r, :] = cot_v[r, k * 128:(k + 1) * 128].astype(F32)
        cotf_out[3, r, :] = jnp.zeros((48, 128), F32)
        cotf_out[3, r, :OFF] = cot_v[r, LT:].astype(F32)
        return 0
    lax.fori_loop(0, B * T // 48, prep, 0)
    col48 = lax.broadcasted_iota(jnp.int32, (B, B), 1)
    row48 = lax.broadcasted_iota(jnp.int32, (B, B), 0)
    def turn(col):
        return jnp.sum(jnp.where(col48 == row48, jnp.broadcast_to(col, (B, B)), 0.0), 0, keepdims=True)
    ln = jnp.broadcast_to(len_v[...], (B, B)).astype(F32)
    key = ln * 64.0 + (B - 1 - col48).astype(F32)
    kcol = jnp.sum(jnp.where(col48 == row48, key, 0.0), 1, keepdims=True)
    rank = jnp.sum(jnp.where(kcol > key, 1.0, 0.0), 0, keepdims=True)
    hit = jnp.broadcast_to(rank, (B, B)) == row48.astype(F32)
    lcol = jnp.sum(jnp.where(hit, ln, 0.0), 1, keepdims=True)
    lens_out[...] = jnp.broadcast_to(lcol, (B, 128))
    most = jnp.zeros((B, 1), F32)
    row1 = lax.broadcasted_iota(jnp.int32, (B, 1), 0)
    for g, end in enumerate(PLANS[0]):
        most = jnp.where(row1 // SUB == g, float(end), most)
    fits = jnp.where(jnp.max(lcol - most, 0, keepdims=True) > 0.0, 0.0, 1.0)
    info_out[...] = jnp.zeros((SUB, 128), jnp.int32)
    info_out[0:1, :B] = rank.astype(jnp.int32)
    info_out[1:2, :B] = turn(jnp.sum(jnp.where(hit, col48.astype(F32), 0.0), 1, keepdims=True)).astype(jnp.int32)
    info_out[2:3, :B] = jnp.broadcast_to(fits, (1, B)).astype(jnp.int32)
    for src, out in ((gain_v, gain_out), (shift_v, shift_out)):
        out[...] = jnp.zeros((SUB, HP), F32)
        out[:, :H] = jnp.broadcast_to(src[...], (SUB, H))
    brow[...] = jnp.zeros((SUB, HP), F32)
    brow[:1, :H] = bias_v[...]
    passed = []
    for n in range(2):
        first[n].wait_recv()
        cp = copy(5 + n, xp, *cuts[n], sib)
        cp.start()
        passed.append(cp)
    for cp in first[2:] + passed:
        cp.wait_recv()
    for cp in first + passed:
        cp.wait_send()
    bias = brow[:1, :]
    hi = bias.astype(BF16).astype(F32)
    mid = (bias - hi).astype(BF16).astype(F32)
    lo = bias - hi - mid
    def lay(rows, l):
        b0, b1, b2, b3 = rows
        b1, b2, b3 = pltpu.roll(b1, 100, 1), pltpu.roll(b2, 72, 1), pltpu.roll(b3, 44, 1)
        return [jnp.where(l < 100, b0, b1), jnp.where(l < 72, b1, b2), jnp.where(l < 44, b2, b3), jnp.where(l < 16, b3, 0.0)]
    l80 = lax.broadcasted_iota(jnp.int32, (80, 128), 1)
    for r in range(0, H, 80):
        for k, v in enumerate(lay([blk[k, r:r + 80, :].astype(F32) for k in range(4)], l80)):
            wc_out[r:r + 80, k * 128:(k + 1) * 128] = v.astype(BF16)
    for k in range(4):
        stage[...] = blk[k].astype(F32)
        cst4 = unpack_extra(lambda q: stage[q * XR:(q + 1) * XR, :], lane)
        blk[k, :XR + 8, :] = jnp.concatenate([cst4, jnp.zeros((8, 128), F32)], 0).astype(BF16)
    row = lax.broadcasted_iota(jnp.int32, (HP - H, 128), 0)
    l112 = lax.broadcasted_iota(jnp.int32, (HP - H, 128), 1)
    for k, v in enumerate(lay([blk[k, :HP - H, :].astype(F32) for k in range(4)], l112)):
        for n, part in enumerate((hi, mid, lo)):
            v = jnp.where(row == E + n, jnp.broadcast_to(part[:, k * 128:(k + 1) * 128], (HP - H, 128)), v)
        wc_out[H:, k * 128:(k + 1) * 128] = v.astype(BF16)


def gather_call(w, c, bias, lengths, x, cot, gain, shift):
    D = pltpu.SemaphoreType.DMA
    V = pltpu.VMEM
    S = jax.ShapeDtypeStruct
    return pl.pallas_call(
        gather_body,
        out_shape=(S((HP, HP), BF16), S((SUB, 128), jnp.int32), S((B, 128), F32), S((B * T, 128), F32), S((NT, B * T, 128), F32), S((SUB, HP), F32), S((SUB, HP), F32)),
        in_specs=[pl.BlockSpec(memory_space=pltpu.HBM)] * 8,
        scratch_shapes=[V((H, E), BF16), V((E, E), BF16), V((1, H), F32), V((1, B), jnp.int32), V((B * T, E), BF16), V((B * T, H), BF16),
            V((1, H), F32), V((1, H), F32),
            V((4, PR, 128), BF16), V((PR, 128), F32), V((XR, 128), F32), V((SUB, HP), F32), V((48, 128), F32), D((7,)), D((7,)), D((8,))],
        compiler_params=pltpu.CompilerParams(collective_id=0, has_side_effects=True, vmem_limit_bytes=12 * 2**20),
    )(*[pltpu.with_memory_space_constraint(v, pltpu.HBM) for v in (
        w, c, bias.reshape(1, H), lengths.reshape(1, B), x.reshape(B * T, E), cot.reshape(B * T, H), gain.reshape(1, H), shift.reshape(1, H))])


OWN = 4
FIRST = 2


def spans():
    tiles = PR // 16
    return tiles // OWN, tiles % OWN


def reduce_body(nb, hx, dp, sums_ref, out_ref, blk, pk, sib_in, rs_out, rs_in, ssem, srsem, rsem_s, rsem_r, asem_s, asem_r):
    me, b = lax.axis_index("tm"), lax.axis_index("batch")
    core, sib, xi = lax.rem(me, 2), lax.bitwise_xor(me, 1), me // 2
    group = b // nb * nb
    rank = b - group
    base, more = spans()
    big, small = (base + 1) * 16, base * 16
    barrier = pltpu.get_barrier_semaphore()
    pl.semaphore_signal(barrier, inc=1, device_id=(sib, b), device_id_type=MESH)
    others = [(dx, db) for db in range(nb) for dx in range(2) if dx or db]
    for dx, db in others:
        pl.semaphore_signal(barrier, inc=1, device_id=(2 * lax.rem(xi + dx, 2) + core, group + lax.rem(rank + db, nb)), device_id_type=MESH)
    def blocks(t, l):
        t0, t1, t2, t3 = t
        return [t0,
            jnp.where(l < 28, pltpu.roll(t0, 28, 1), pltpu.roll(t1, 28, 1)),
            jnp.where(l < 56, pltpu.roll(t1, 56, 1), pltpu.roll(t2, 56, 1)),
            jnp.where(l < 84, pltpu.roll(t2, 84, 1), pltpu.roll(t3, 84, 1))]
    gsum = jnp.sum(sums_ref[:SUB, :], 0, keepdims=True)
    ssum = jnp.sum(sums_ref[SUB:, :], 0, keepdims=True)
    l128 = lax.broadcasted_iota(jnp.int32, (128, 128), 1)
    r128 = lax.broadcasted_iota(jnp.int32, (128, 128), 0)
    for m in range(4):
        prod = lax.dot_general(hx[:, m * 128:(m + 1) * 128], dp[...], (((0,), (0,)), ((), ())), preferred_element_type=F32)
        t = [prod[:, k * 128:(k + 1) * 128] for k in range(4)]
        if m == 3:
            for k in range(4):
                gk = jnp.broadcast_to(gsum[:, k * 128:(k + 1) * 128], (128, 128))
                sk = jnp.broadcast_to(ssum[:, k * 128:(k + 1) * 128], (128, 128))
                t[k] = jnp.where(r128 == OFF + E + 1, gk, jnp.where(r128 == OFF + E + 2, sk, t[k]))
        for k, v in enumerate(blocks(t, l128)):
            blk[k, m * 128:(m + 1) * 128, :] = v
    lane = lax.broadcasted_iota(jnp.int32, (XR, 128), 1)
    for k in range(4):
        extra = blk[k, H:H + XR, :]
        blk[k, H:H + 16, :] = jnp.zeros((16, 128), F32)
        for q, p in enumerate(pack(lambda q: blk[k, q * XR:(q + 1) * XR, :], extra, lane)):
            blk[k, q * XR:(q + 1) * XR, :] = p
        pk[k] = blk[k, :PR, :].astype(BF16)
    pl.semaphore_wait(barrier, len(others) + 1)
    scopies = []
    for j in range(2):
        cp = pltpu.make_async_remote_copy(src_ref=pk.at[2 * j + (1 - core)], dst_ref=sib_in.at[j], send_sem=ssem.at[j], recv_sem=srsem.at[j],
            device_id=(sib, b), device_id_type=MESH)
        cp.start()
        scopies.append(cp)
    def sized(owner, run):
        pl.when(owner < more)(lambda: run(big))
        pl.when(owner >= more)(lambda: run(small))
    def span(owner, rows):
        return pl.ds(pl.multiple_of((owner * base + lax.min(owner, more)) * 16, 16), rows)
    mine = xi * nb + rank
    owner = rank - FIRST
    is_owner = (owner >= 0) & (owner < OWN)
    far = 2 - 2 * (rank // (nb // 2))
    def rcopy(px, o, rows):
        n = px * OWN + o
        return pltpu.make_async_remote_copy(src_ref=rs_out.at[px, span(o, rows)], dst_ref=rs_in.at[mine, pl.ds(0, rows)],
            send_sem=rsem_s.at[n], recv_sem=rsem_r.at[mine], device_id=(2 * px + core, group + FIRST + o), device_id_type=MESH)
    def arrived(slot, rows):
        return pltpu.make_async_remote_copy(src_ref=rs_out.at[0, pl.ds(0, rows)], dst_ref=rs_in.at[slot, pl.ds(0, rows)],
            send_sem=rsem_s.at[0], recv_sem=rsem_r.at[slot], device_id=(2 * (1 - xi) + core, b), device_id_type=MESH)
    def targets():
        for px in range(2):
            for n in range(OWN):
                o = lax.rem(far + n, OWN)
                yield px, o, (px != xi) | (o != owner)
    def acopy(db, o, rows):
        return pltpu.make_async_remote_copy(src_ref=out_ref.at[span(o, rows)], dst_ref=out_ref.at[span(o, rows)], send_sem=asem_s.at[db],
            recv_sem=asem_r.at[o], device_id=(me, group + lax.rem(rank + db, nb)), device_id_type=MESH)
    for j in range(2):
        scopies[j].wait_recv()
        rs_out[j] = (blk[2 * j + core, :PR, :] + sib_in[j].astype(F32)).astype(BF16)
        for px, o, other in targets():
            if px == j:
                pl.when(other)(lambda px=px, o=o: sized(o, lambda rows: rcopy(px, o, rows).start()))
    def collect(rows):
        total = rs_out[xi, span(owner, rows), :].astype(F32)
        for n in range(1, 2 * nb):
            slot = lax.rem(mine + n, 2 * nb)
            arrived(slot, rows).wait_recv()
            total = total + rs_in[slot, :rows, :].astype(F32)
        out_ref[span(owner, rows), :] = total.astype(BF16)
        for db in range(1, nb):
            acopy(db, owner, rows).start()
    pl.when(is_owner)(lambda: sized(owner, collect))
    for o in range(OWN):
        rows = big if o < more else small
        pl.when(owner != o)(lambda o=o, rows=rows: acopy(1, o, rows).wait_recv())
    for cp in scopies:
        cp.wait_send()
    for px, o, other in targets():
        pl.when(other)(lambda px=px, o=o: sized(o, lambda rows: rcopy(px, o, rows).wait_send()))
    def sent(rows):
        for db in range(1, nb):
            acopy(db, owner, rows).wait_send()
    pl.when(is_owner)(lambda: sized(owner, sent))


def reduce_call(hx, dp, sums, nb):
    D = pltpu.SemaphoreType.DMA
    V = pltpu.VMEM
    vs = pl.BlockSpec(memory_space=pltpu.VMEM)
    big = (spans()[0] + 1) * 16
    return pl.pallas_call(
        functools.partial(reduce_body, nb),
        out_shape=jax.ShapeDtypeStruct((PR, 128), BF16),
        in_specs=[vs, vs, vs],
        out_specs=vs,
        scratch_shapes=[V((4, HP, 128), F32), V((4, PR, 128), BF16), V((2, PR, 128), BF16),
            V((2, PR, 128), BF16), V((2 * nb, big, 128), BF16),
            D((2,)), D((2,)), D((2 * OWN,)), D((2 * nb,)), D((nb,)), D((OWN,))],
        compiler_params=pltpu.CompilerParams(collective_id=1, has_side_effects=True, vmem_limit_bytes=16 * 2**20),
    )(hx, dp, sums)


def spread_body(p_ref, gw_out, gc_out, gb_out, gg_out, gs_out, stage):
    stage[...] = p_ref[...].astype(F32)
    gw_out[...] = stage[:H, :E]
    lane = lax.broadcasted_iota(jnp.int32, (XR, 128), 1)
    extra = unpack_extra(lambda q: stage[q * XR:(q + 1) * XR, :], lane)
    stage[:XR, :] = extra
    gc_out[...] = stage[:E, :E]
    for n, ref in enumerate((gb_out, gg_out, gs_out)):
        ref[...] = stage[E + n:E + n + 1, :E]


def spread_call(p):
    S = jax.ShapeDtypeStruct
    vec = S((1, E), F32)
    return pl.pallas_call(
        spread_body,
        out_shape=(S((H, E), F32), S((E, E), F32), vec, vec, vec),
        scratch_shapes=[pltpu.VMEM((PR, 128), F32)],
        compiler_params=pltpu.CompilerParams(vmem_limit_bytes=8 * 2**20),
    )(p)


def per_device(inputs, lengths, w_rec, w_in, rec_bias, norm_gain, norm_shift, cotangent, nb):
    wc, info, lens, xs, cotf, gain, shift = gather_call(w_rec, w_in, rec_bias, lengths, inputs, cotangent, norm_gain, norm_shift)
    hid, gx, hx, dp, sums = cell_call(info, xs, lens, cotf, wc, gain, shift)
    group = math.gcd(nb, 8)
    p = reduce_call(hx, dp, sums, group)
    if nb > group:
        p = lax.all_gather(p.astype(F32), "batch").reshape(nb // group, group, PR, 128)[:, 0].sum(0)
    gw, gc, gb, gg, gs = spread_call(p)
    return hid.reshape(B, T, H), gx.reshape(B, T, E), gw, gc, gb.reshape(E), gg.reshape(E), gs.reshape(E)


def solution(mesh):
    both = ("tm", "batch")
    return jax.shard_map(
        functools.partial(per_device, nb=mesh.shape["batch"]),
        mesh=mesh,
        in_specs=(P(both, None, None), P(both), P(None, "tm"), P(None, "tm"), P(), P(), P(), P(both, None, None)),
        out_specs=(P(both, None, None), P(both, None, None), P(None, "tm"), P(None, "tm"), P("tm"), P("tm"), P("tm")),
        check_vma=False,
    )
```
